32 devices in a mesh: blk: 2 (over core), span: 4 (over y, x), inst: 4 (over z).
Axes of the slice: x: 2, y: 2, z: 4, core: 2. Of those that a mesh axis runs over, the one named last changes fastest.
Arguments:
- source: bfloat16 [4, 16, 81920], P('inst', None, ('blk', 'span')), may hold values from -6 to 6
- jac_interior: bfloat16 [32, 10, 320, 320], P(('blk', 'span', 'inst')), may hold values from -0.25 to 0.25
- interior_rows: int32 [32, 10], P(('blk', 'span', 'inst')), may hold values from 0 to 31
- interior_cols: int32 [32, 10], P(('blk', 'span', 'inst')), may hold values from 0 to 31
- jac_face: bfloat16 [32, 8, 320, 320], P(('blk', 'span', 'inst')), may hold values from -0.25 to 0.25
- face_rows: int32 [32, 8], P(('blk', 'span', 'inst')), may hold values from 0 to 31
- face_cols: int32 [32, 8], P(('blk', 'span', 'inst')), may hold values from 0 to 7, each once within a row
- face_map: int32 [4], replicated, may hold values from 0 to 3, each once
- frequency: float32 [1], replicated, may hold values from 0.04 to 0.1
- surf_mode: int32 [8192, 1], P(('blk', 'span', 'inst')), may hold values from 0 to 1; in each aligned block of 256 rows (0 to 255, 256 to 511, ...) at most 256 rows name the same one
- surf_row: int32 [32, 256], P(('blk', 'span', 'inst')), may hold values from 0 to 10239
- surf_node: int32 [32, 256], P(('blk', 'span', 'inst')), may hold values from 0 to 32767
- mode_shape: float32 [2, 32768], P('blk'), may hold values from -0.4375 to 0.4375
Outputs:
- adjoint: bfloat16 [4, 16, 81920], P('inst', None, ('blk', 'span'))
- modal_grad: float32 [4, 2, 16], P('inst', 'blk')
The draws below stay inside these ranges and needn't reach their ends.
Inputs may be any that keep to these rules, and one draw needn't show every extreme that they name: `surf_mode`: within the 256 entries of one device no mode is named by more than 256 entries, a bound that some block reaches. `face_cols`: each row names every number below 8 once. `face_map`: each number below 4 once.
All inputs are finite; a program needn't handle non-finite values.
Results may differ from the reference program's by a relative error of at most 0.0051.
Values may be sent and summed in bfloat16 or wider, within the bound.
A program may use at most 64 MiB of HBM per device.

```python
import math
import jax
import jax.numpy as jnp
import numpy as np
from jax import lax

BS = 320
RHS = 16
MODES = 2
NB = 32
NI = 10
FB = 2
NF = 8
PF = 4
ITERS = 6
SURF = 256
CAP = 256
SURF_NODES = 32768
N_BLK = 2
N_SPAN = 4
N_INST = 4


def plant(result, stream_key, least, top_value):
    place = [jax.random.randint(jax.random.fold_in(stream_key, axis), (), 0, length) for axis, length in enumerate(result.shape)]
    widest = result.shape.index(max(result.shape))
    next_to = place[:widest] + [(place[widest] + 1) % result.shape[widest]] + place[widest + 1:]
    return result.at[tuple(place)].set(least).at[tuple(next_to)].set(top_value)


def block_levels(key, extent, cuts, low, high):
    def one(axis_at, shards_of):
        steps = jax.random.uniform(jax.random.fold_in(jax.random.fold_in(key, 6), axis_at), (shards_of,), jnp.float32, low / len(cuts), high / len(cuts))
        return jnp.repeat(jnp.exp(steps), extent[axis_at] // shards_of).reshape((-1,) + (1,) * (len(extent) - axis_at - 1))

    level = one(*cuts[0])
    for cut in cuts[1:]:
        level = level * one(*cut)
    return level


def shared_out(key, own, number, rows, count, top, bound, skew):
    order = jax.random.permutation(key, count)
    packed, usual = portions_of(count, rows * top, bound, skew, True), portions_of(count, rows * top, bound, skew, False)
    places = jnp.arange(count)

    def named(tallies, turn):
        used = int((tallies > 0).sum())
        fixed = max(1, used // 4)
        shifted = fixed + (places - fixed + turn * (used - fixed)) % max(1, count - fixed)
        return jnp.zeros((count,), jnp.int32).at[order[jnp.where(places < fixed, places, shifted)]].set(jnp.asarray(tallies, jnp.int32))

    tallies = jnp.where(number % 4 == 0, named(packed, number // 4), named(usual, number - number // 4 - 1))
    mixed = jax.random.permutation(jax.random.fold_in(own, 3), count)
    source_of, sink = mixed[0:count // 2 * 2:2], mixed[1:count // 2 * 2:2]
    margin = jnp.minimum(tallies[source_of] - 1, bound - tallies[sink]) // 2
    margin = jnp.where((source_of == order[0]) | (sink == order[0]) | (tallies[sink] == 0), 0, jnp.maximum(margin, 0))
    shifted = jax.random.randint(jax.random.fold_in(own, 4), (count // 2,), 0, 1 << 20) % (margin + 1)
    tallies = tallies.at[source_of].add(-shifted).at[sink].add(shifted)
    labels = jnp.searchsorted(jnp.cumsum(tallies), jnp.arange(rows * top), side="right").astype(jnp.int32)
    listing = labels.reshape(top, rows).T
    listing = listing[jax.random.permutation(jax.random.fold_in(own, 1), rows)]
    turn = jax.random.randint(jax.random.fold_in(own, 2), (rows, 1), 0, top)
    return jnp.take_along_axis(listing, (jnp.arange(top)[None, :] + turn) % top, axis=1)


def portions_of(amount, total, reach, slope, full):
    weights = [(1 << 20) // math.isqrt(standing ** slope) + 1 for standing in range(1, amount + 1)]
    largest = reach if full else min(reach, max(-(-total // amount), total * weights[0] // sum(weights)))
    least = 1 if total - largest >= amount - 1 else 0
    given, surplus = [largest] + [least] * (amount - 1), total - largest - least * (amount - 1)
    while surplus > 0:
        candidates = [i for i in range(1, amount) if given[i] < largest] or [i for i in range(1, amount) if given[i] < reach]
        whole, budget = sum([weights[i] for i in candidates]), surplus
        for i in candidates:
            more = min(reach - given[i], max(1, budget * weights[i] // whole), surplus)
            given[i] = given[i] + more
            surplus = surplus - more
    return np.array(given)


def bell_draw(stream_key, extent, deviation, limit, pieces=(), kind=jnp.bfloat16):
    entries = jax.random.normal(stream_key, extent, jnp.float32) * deviation
    if len(pieces) > 0:
        entries = block_levels(stream_key, extent, pieces, -0.22, 0.18) * entries
    return jnp.clip(entries, min=-limit, max=limit).astype(kind)


def setup_inputs(seed: int = 0) -> dict:
    splits = jax.random.split(jax.random.key(seed), 14)
    source = bell_draw(splits[0], (N_INST, RHS, N_BLK * N_SPAN * NB * BS), 1.0, 6.0, ((0, 4), (2, 8)))
    jac_interior = bell_draw(splits[1], (N_BLK * N_SPAN * N_INST, NI, BS, BS), (2 * BS) ** -0.5, 0.25, ((0, 32),))
    interior_rows = plant(jax.random.randint(splits[2], (N_BLK * N_SPAN * N_INST, NI), 0, NB), jax.random.fold_in(splits[2], 1), 0, NB - 1).astype(jnp.int32)
    interior_cols = plant(jax.random.randint(splits[3], (N_BLK * N_SPAN * N_INST, NI), 0, NB), jax.random.fold_in(splits[3], 1), 0, NB - 1).astype(jnp.int32)
    jac_face = bell_draw(splits[4], (N_BLK * N_SPAN * N_INST, NF, BS, BS), (2 * BS) ** -0.5, 0.25, ((0, 32),))
    face_rows = plant(jax.random.randint(splits[5], (N_BLK * N_SPAN * N_INST, NF), 0, NB), jax.random.fold_in(splits[5], 1), 0, NB - 1).astype(jnp.int32)
    face_cols = jax.vmap(lambda own: jax.random.permutation(own, NF))(jax.random.split(splits[6], (N_BLK * N_SPAN * N_INST))).reshape((N_BLK * N_SPAN * N_INST, NF)).astype(jnp.int32)
    face_map = jax.random.permutation(splits[7], PF).astype(jnp.int32)
    frequency = jnp.clip(jax.random.uniform(splits[8], (1,), jnp.float32, 0.04, 0.1), 0.04, 0.1)
    surf_mode_keys = jax.random.split(jax.random.fold_in(splits[9], 1), (N_BLK * N_SPAN * N_INST * SURF) // SURF)
    surf_mode_turns = jax.random.permutation(jax.random.fold_in(splits[9], 3), (N_BLK * N_SPAN * N_INST * SURF) // SURF)
    surf_mode = jax.vmap(lambda own, number: shared_out(jax.random.fold_in(splits[9], 2), own, number, SURF, MODES, 1, CAP, 2))(surf_mode_keys, surf_mode_turns).reshape((N_BLK * N_SPAN * N_INST * SURF, 1))
    surf_row = plant(jax.random.randint(splits[10], (N_BLK * N_SPAN * N_INST, SURF), 0, NB * BS), jax.random.fold_in(splits[10], 1), 0, (NB * BS) - 1).astype(jnp.int32)
    surf_node = plant(jax.random.randint(splits[11], (N_BLK * N_SPAN * N_INST, SURF), 0, SURF_NODES), jax.random.fold_in(splits[11], 1), 0, SURF_NODES - 1).astype(jnp.int32)
    mode_shape = bell_draw(splits[12], (MODES, SURF_NODES), 0.03, 0.4375, ((0, 2),), jnp.float32)
    return {"source": source, "jac_interior": jac_interior, "interior_rows": interior_rows, "interior_cols": interior_cols, "jac_face": jac_face, "face_rows": face_rows, "face_cols": face_cols, "face_map": face_map, "frequency": frequency, "surf_mode": surf_mode, "surf_row": surf_row, "surf_node": surf_node, "mode_shape": mode_shape}


def loop_weight(offset, inst_count):
    angle = math.pi * offset / inst_count
    parity = jnp.cos(math.pi * offset)
    sine_safe = jnp.where(offset == 0, 1.0, jnp.sin(angle))
    value = 0.5 * parity / sine_safe
    return jnp.where(offset == 0, 0.0, value)


def device_sweep(operands):
    own_blocks, face_sources, jac_in, rows_in, cols_in, jac_out, rows_out, cols_out = operands
    inner_prod = jnp.einsum('rnk,nkl->rnl', own_blocks[:, cols_in, :].astype(jnp.float32), jac_in.astype(jnp.float32), precision=lax.Precision.HIGHEST)
    outer_prod = jnp.einsum('rnk,nkl->rnl', face_sources[:, cols_out, :].astype(jnp.float32), jac_out.astype(jnp.float32), precision=lax.Precision.HIGHEST)
    summed = jnp.zeros(own_blocks.shape, jnp.float32).at[:, rows_in, :].add(inner_prod)
    return summed.at[:, rows_out, :].add(outer_prod)


def reference(source, jac_interior, interior_rows, interior_cols, jac_face, face_rows, face_cols, face_map, frequency, surf_mode, surf_row, surf_node, mode_shape):
    device_count = N_BLK * N_SPAN * N_INST
    shaped = (N_INST, RHS, N_BLK, N_SPAN, NB, BS)
    source_wide = source.astype(jnp.float32)
    offsets = jnp.arange(N_INST).astype(jnp.float32)
    loop_matrix = loop_weight(offsets[:, None] - offsets[None, :], N_INST)
    psi_now = source
    for sweep_step in range(ITERS):
        grid = psi_now.reshape(shaped)
        spectral = jnp.einsum('ji,jrc->irc', loop_matrix, psi_now.astype(jnp.float32), precision=lax.Precision.HIGHEST)
        prev_face = jnp.roll(grid[:, :, :, :, NB - FB:, :], 1, axis=2)
        next_face = jnp.roll(grid[:, :, :, :, :FB, :], -1, axis=2)
        passage = jnp.concatenate([prev_face, next_face], axis=4)[:, :, :, :, face_map, :]
        empty_slab = jnp.zeros_like(grid[:, :, :, :1, :FB, :])
        lower_rim = jnp.concatenate([empty_slab, grid[:, :, :, :-1, NB - FB:, :]], axis=3)
        upper_rim = jnp.concatenate([grid[:, :, :, 1:, :FB, :], empty_slab], axis=3)
        face_sources = jnp.concatenate([passage, lower_rim, upper_rim], axis=4)
        own_dev = grid.transpose(2, 3, 0, 1, 4, 5).reshape(device_count, RHS, NB, BS)
        face_dev = face_sources.transpose(2, 3, 0, 1, 4, 5).reshape(device_count, RHS, 4 * FB, BS)
        summed = lax.map(device_sweep, (own_dev, face_dev, jac_interior, interior_rows, interior_cols, jac_face, face_rows, face_cols))
        summed = summed.reshape(N_BLK, N_SPAN, N_INST, RHS, NB, BS).transpose(2, 3, 0, 1, 4, 5).reshape(source.shape)
        psi_now = (source_wide - summed - frequency[0] * spectral).astype(jnp.bfloat16)
    flat_dev = psi_now.reshape(N_INST, RHS, N_BLK, N_SPAN, NB * BS).transpose(2, 3, 0, 1, 4).reshape(device_count, RHS, NB * BS)
    loads = jnp.take_along_axis(flat_dev, surf_row[:, None, :], axis=2).astype(jnp.float32)
    modes_dev = surf_mode.reshape(device_count, SURF)
    picked = mode_shape[modes_dev, surf_node]
    terms = (loads * picked[:, None, :]).transpose(0, 2, 1)
    inst_of = jnp.broadcast_to((jnp.arange(device_count) % N_INST).astype(jnp.int32)[:, None], (device_count, SURF))
    modal_grad = jnp.zeros((N_INST, MODES, RHS), jnp.float32).at[inst_of, modes_dev].add(terms)
    return psi_now, modal_grad
```

```python
import functools
import math

import jax
import jax.numpy as jnp
import numpy as np
from jax import lax
from jax.experimental import pallas as pl
from jax.experimental.pallas import tpu as pltpu
from jax.sharding import PartitionSpec as P

ITERS = 6
F32 = jnp.float32
BF16 = jnp.bfloat16


def sweep_kernel(dims, src_ref, jin, jout, icols, fcols, fmap, prev, freq, wt, last_ref, wm_ref,
                 out_ref, mod_ref,
                 srcg, srcb, psi, acc, uown, ugot, faces, lastg, lasts, part, partg,
                 floc, uloc, src_s, src_r, last_s, last_r, loc_sem, face_s, face_r, u_s, u_r, mod_s, mod_r):
    n, nblk, nspan, ni, nf, nb, bs = dims
    blk, span, me = lax.axis_index("blk"), lax.axis_index("span"), lax.axis_index("inst")
    entries = ni + nf

    def inst_peer(d):
        return {"inst": lax.rem(me + d, n)}

    def ring_peer(db, ds):
        return {"blk": lax.rem(blk + db, nblk), "span": lax.rem(span + ds, nspan)}

    others = [(db, ds) for db in range(nblk) for ds in range(nspan) if db or ds]
    barrier = pltpu.get_barrier_semaphore()
    for d in range(1, n):
        pl.semaphore_signal(barrier, inc=1, device_id=inst_peer(d), device_id_type=pl.DeviceIdType.MESH)
    for db, ds in others:
        pl.semaphore_signal(barrier, inc=1, device_id=ring_peer(db, ds), device_id_type=pl.DeviceIdType.MESH)
    pl.semaphore_wait(barrier, n - 1 + len(others))

    def remote(src, dst, send, recv, peer):
        return pltpu.make_async_remote_copy(src_ref=src, dst_ref=dst, send_sem=send, recv_sem=recv,
                                            device_id=peer, device_id_type=pl.DeviceIdType.MESH)

    def last_copy(d):
        return remote(last_ref, lastg.at[n - d - 1], last_s.at[d - 1], last_r.at[n - d - 1], inst_peer(d))

    def src_copy(d):
        return remote(src_ref, srcg.at[n - d - 1], src_s.at[d - 1], src_r.at[n - d - 1], inst_peer(d))

    def u_copy(t, d):
        return remote(uown.at[t], ugot.at[t, n - d - 1], u_s.at[t, d - 1], u_r.at[t, n - d - 1], inst_peer(d))

    def u_wait(t, d):
        remote(uown.at[t], ugot.at[t, d - 1], u_s.at[t, n - d - 1], u_r.at[t, d - 1], inst_peer(d)).wait_recv()
        uloc[d - 1] = ugot[t, d - 1]

    def face_copies(t, par):
        head, tail = psi.at[par, 0, pl.ds(0, 2)], psi.at[par, 0, pl.ds(nb - 2, 2)]
        plan = ((tail, 1, 0), (head, nblk - 1, 0), (tail, 0, 1), (head, 0, nspan - 1))
        return [remote(part_, faces.at[t, k], face_s.at[t, k], face_r.at[t, k], ring_peer(db, ds))
                for k, (part_, db, ds) in enumerate(plan)]

    for d in range(1, n):
        last_copy(d).start()
    for d in range(1, n):
        src_copy(d).start()

    acc[entries] = jnp.zeros_like(acc[entries])

    def relayout(ref, d):
        def body(q, carry):
            pair = ref[:, pl.ds(pl.multiple_of(q * 2 * bs, 128), 2 * bs)]
            srcb[d, 2 * q] = pair[:, :bs]
            srcb[d, 2 * q + 1] = pair[:, bs:]
            return carry
        lax.fori_loop(0, nb // 2, body, 0)

    relayout(src_ref, 0)

    def own_copy(b, carry):
        psi[0, 0, b] = srcb[0, b]
        return carry
    lax.fori_loop(0, nb, own_copy, 0)

    rate = freq[0]

    def weight(di, dj):
        k = lax.rem(me + dj, n) - lax.rem(me + di, n)
        return rate * wt[k + n - 1]

    def products(t, par):
        sends = face_copies(t, par)
        for copy in sends:
            copy.start()
        for e in range(ni):
            x = psi[par, 0, icols[0, e]]
            prod = jnp.dot(x, jin[e], preferred_element_type=F32)
            acc[e] = prod + acc[prev[e]]
        for k, copy in enumerate(sends):
            copy.wait()
            floc[2 * k] = faces[t, k, 0]
            floc[2 * k + 1] = faces[t, k, 1]
        for e in range(nf):
            c = fcols[0, e]
            c = jnp.where(c < 4, fmap[jnp.minimum(c, 3)], c)
            beyond = ((c >= 4) & (c < 6) & (span == 0)) | ((c >= 6) & (span == nspan - 1))
            keep = jnp.where(beyond, 0.0, 1.0)
            x = floc[c]
            prod = jnp.dot(x, jout[e], preferred_element_type=F32) * keep
            acc[ni + e] = prod + acc[prev[ni + e]]

    def send_u(t):
        for e in range(entries):
            uown[t, e] = acc[e].astype(BF16)
        for d in range(1, n):
            u_copy(t, d).start()

    def block(t, par, b, first, final):
        nxt = 1 - par
        if first:
            now = [srcb[d, b].astype(F32) for d in range(1, n)]
        else:
            old = [psi[nxt, d, b].astype(F32) for d in range(n)]
            now = []
            for d in range(1, n):
                at = lasts[d - 1, 0, b]
                got = uloc[d - 1, jnp.minimum(at, entries - 1)].astype(F32)
                val = srcb[d, b].astype(F32) - jnp.where(at < entries, got, 0.0)
                for j in range(n):
                    if j != d:
                        val = val - weight(d, j) * old[j]
                val = val.astype(BF16)
                if not final:
                    psi[par, d, b] = val
                now.append(val.astype(F32))
        if first:
            for d in range(1, n):
                psi[par, d, b] = srcb[d, b]
        val = srcb[0, b].astype(F32) - acc[own_last(b)]
        spec = weight(0, 1) * now[0]
        for d in range(2, n):
            spec = spec + weight(0, d) * now[d - 1]
        val = (val - spec).astype(BF16)
        psi[nxt, 0, b] = val
        return val

    def own_last(b):
        return lasts[n - 1, 0, b]

    def update(t, par, first=False, final=False):
        def body(q, carry):
            lo = block(t, par, 2 * q, first, final)
            hi = block(t, par, 2 * q + 1, first, final)
            if final:
                out_ref[:, pl.ds(pl.multiple_of(q * 2 * bs, 128), 2 * bs)] = jnp.concatenate([lo, hi], axis=1)
                res = []
                for m in range(nblk):
                    tot = carry[m]
                    tot = tot + lo.astype(F32) * wm_ref[2 * q, m:m + 1, :]
                    tot = tot + hi.astype(F32) * wm_ref[2 * q + 1, m:m + 1, :]
                    res.append(tot)
                return tuple(res)
            return carry
        init = tuple(jnp.zeros((src_ref.shape[0], bs), F32) for _ in range(nblk)) if final else 0
        return lax.fori_loop(0, nb // 2, body, init)

    products(0, 0)
    send_u(0)
    for d in range(1, n):
        last_copy(d).wait()
        src_copy(d).wait()
    local = [pltpu.make_async_copy(last_ref, lasts.at[n - 1], loc_sem.at[n - 1])]
    local += [pltpu.make_async_copy(lastg.at[d - 1], lasts.at[d - 1], loc_sem.at[d - 1]) for d in range(1, n)]
    for copy in local:
        copy.start()
    for copy in local:
        copy.wait()
    for d in range(1, n):
        relayout(srcg.at[d - 1], d)
    update(0, 0, first=True)

    def sweep(t, carry):
        par = lax.rem(t, 2)
        products(t, par)
        send_u(t)
        for d in range(1, n):
            u_wait(t - 1, d)
        update(t, par)
        return carry

    lax.fori_loop(1, ITERS - 1, sweep, 0)
    t_end = ITERS - 1
    products(t_end, t_end % 2)
    for d in range(1, n):
        u_wait(t_end - 1, d)
    totals = update(t_end, t_end % 2, final=True)

    for m in range(nblk):
        part[m] = jnp.broadcast_to(jnp.sum(totals[m], axis=1, keepdims=True), part.shape[1:])

    def slot(db, ds):
        return db * nspan + ds - 1

    copies = []
    for db, ds in others:
        mine = slot(db, ds)
        theirs = slot((nblk - db) % nblk, (nspan - ds) % nspan)
        copies.append(remote(part.at[lax.rem(blk + db, nblk)], partg.at[theirs], mod_s.at[mine], mod_r.at[theirs],
                             ring_peer(db, ds)))
    for copy in copies:
        copy.start()
    for copy in copies:
        copy.wait_send()
    total = part[blk]
    for k in range(len(others)):
        copies[k].wait_recv()
    for k in range(len(others)):
        total = total + partg[k]
    mod_ref[...] = total

    def drain(t, carry):
        for d in range(1, n):
            u_copy(t, d).wait_send()
        return carry
    lax.fori_loop(0, ITERS - 1, drain, 0)


def modal_weights(surf_mode, surf_row, surf_node, mode_shape, columns, bs):
    nblk = lax.axis_size("blk")
    lanes = 128
    shapes = lax.all_gather(mode_shape[0], "blk", axis=0, tiled=False)
    nodes = shapes.shape[1]
    e_node, e_row, e_mode = surf_node[0], surf_row[0], surf_mode[:, 0]
    hi = (e_node[:, None] // lanes == jnp.arange(nodes // lanes)[None]).astype(F32)
    lo = (e_node[:, None] % lanes == jnp.arange(lanes)[None]).astype(F32)
    hit = (e_mode[:, None] == jnp.arange(nblk)[None]).astype(F32)
    rows = jnp.einsum("eh,mhl->eml", hi, shapes.reshape(nblk, -1, lanes), precision=lax.Precision.HIGHEST)
    val = jnp.sum(rows * lo[:, None, :], axis=2) * hit
    blocks = (e_row[:, None] // bs == jnp.arange(columns // bs)[None]).astype(F32)
    lane = (e_row[:, None] % bs == jnp.arange(bs)[None]).astype(F32)
    left = (blocks[:, :, None] * jnp.pad(val, ((0, 0), (0, 8 - nblk)))[:, None, :]).reshape(e_row.shape[0], -1)
    return jnp.dot(left.T, lane, precision=lax.Precision.HIGHEST).reshape(columns // bs, 8, bs)


def on_device(source, jac_interior, interior_rows, interior_cols, jac_face, face_rows, face_cols, face_map,
              frequency, surf_mode, surf_row, surf_node, mode_shape):
    r, columns = source.shape[1:]
    ni, bs = jac_interior.shape[1:3]
    nf = jac_face.shape[1]
    nb = columns // bs
    entries = ni + nf
    n, nblk, nspan = lax.axis_size("inst"), lax.axis_size("blk"), lax.axis_size("span")
    ks = np.arange(-(n - 1), n)
    wt = np.array([0.0 if k == 0 else 0.5 * (-1.0) ** int(k) / math.sin(math.pi * k / n) for k in ks], np.float32)
    rows = jnp.concatenate([interior_rows[0], face_rows[0]])
    order = jnp.arange(entries)
    same = (rows[:, None] == rows[None, :]) & (order[None, :] < order[:, None])
    prev = jnp.max(jnp.where(same, order[None, :], -1), axis=1)
    prev = jnp.where(prev < 0, entries, prev).astype(jnp.int32)
    named = rows[None, :] == jnp.arange(128)[:, None]
    last = jnp.max(jnp.where(named, order[None, :], -1), axis=1)
    last = jnp.where(last < 0, entries, last).astype(jnp.int32)
    last = jnp.broadcast_to(last[None], (8, 128))
    wm = modal_weights(surf_mode, surf_row, surf_node, mode_shape, columns, bs)
    vmem = pl.BlockSpec(memory_space=pltpu.VMEM)
    smem = pl.BlockSpec(memory_space=pltpu.SMEM)
    dma = pltpu.SemaphoreType.DMA
    peers = nblk * nspan - 1
    adj, mod = pl.pallas_call(
        functools.partial(sweep_kernel, (n, nblk, nspan, ni, nf, nb, bs)),
        out_shape=(jax.ShapeDtypeStruct((r, columns), BF16), jax.ShapeDtypeStruct((r, 128), F32)),
        in_specs=[vmem, vmem, vmem, smem, smem, smem, smem, smem, smem, vmem, vmem],
        out_specs=(vmem, vmem),
        scratch_shapes=[
            pltpu.VMEM((n - 1, r, columns), BF16),
            pltpu.VMEM((n, nb, r, bs), BF16),
            pltpu.VMEM((2, n, nb, r, bs), BF16),
            pltpu.VMEM((entries + 1, r, bs), F32),
            pltpu.VMEM((ITERS - 1, entries, r, bs), BF16),
            pltpu.VMEM((ITERS - 1, n - 1, entries, r, bs), BF16),
            pltpu.VMEM((ITERS, 4, 2, r, bs), BF16),
            pltpu.VMEM((n - 1, 8, 128), jnp.int32),
            pltpu.SMEM((n, 8, 128), jnp.int32),
            pltpu.VMEM((nblk, r, 128), F32),
            pltpu.VMEM((peers, r, 128), F32),
            pltpu.VMEM((nf, r, bs), BF16),
            pltpu.VMEM((n - 1, entries, r, bs), BF16),
            dma((n - 1,)), dma((n - 1,)), dma((n - 1,)), dma((n - 1,)), dma((n,)),
            dma((ITERS, 4)), dma((ITERS, 4)),
            dma((ITERS - 1, n - 1)), dma((ITERS - 1, n - 1)),
            dma((peers,)), dma((peers,)),
        ],
        compiler_params=pltpu.CompilerParams(
            collective_id=0, has_side_effects=True, vmem_limit_bytes=58 * 2**20),
        name="sweeps",
    )(source[0], jac_interior[0], jac_face[0], interior_cols, face_cols, face_map, prev, frequency,
      jnp.asarray(wt), last, wm)
    return adj[None], mod[:, 0][None, None]


def solution(mesh):
    dev = ("blk", "span", "inst")
    return jax.shard_map(
        on_device,
        mesh=mesh,
        in_specs=(
            P("inst", None, ("blk", "span")),
            P(dev, None, None, None),
            P(dev, None),
            P(dev, None),
            P(dev, None, None, None),
            P(dev, None),
            P(dev, None),
            P(),
            P(),
            P(dev, None),
            P(dev, None),
            P(dev, None),
            P("blk", None),
        ),
        out_specs=(P("inst", None, ("blk", "span")), P("inst", "blk", None)),
        check_vma=False,
    )
```

```python
import functools
import math

import jax
import jax.numpy as jnp
import numpy as np
from jax import lax
from jax.experimental import pallas as pl
from jax.experimental.pallas import tpu as pltpu
from jax.sharding import PartitionSpec as P

ITERS = 6
F32 = jnp.float32
BF16 = jnp.bfloat16


def sweep_kernel(dims, src_ref, jin, jout, icols, fcols, fmap, prev, freq, wt, last_ref, wm_ref,
                 out_ref, mod_ref,
                 srcg, srcb, psi, acc, uown, ugot, faces, lastg, lasts, part, partg,
                 floc, uloc, src_s, src_r, last_s, last_r, loc_sem, face_s, face_r, u_s, u_r, mod_s, mod_r):
    n, nblk, nspan, ni, nf, nb, bs = dims
    blk, span, me = lax.axis_index("blk"), lax.axis_index("span"), lax.axis_index("inst")
    entries = ni + nf

    def inst_peer(d):
        return {"inst": lax.rem(me + d, n)}

    def ring_peer(db, ds):
        return {"blk": lax.rem(blk + db, nblk), "span": lax.rem(span + ds, nspan)}

    others = [(db, ds) for db in range(nblk) for ds in range(nspan) if db or ds]
    barrier = pltpu.get_barrier_semaphore()
    for d in range(1, n):
        pl.semaphore_signal(barrier, inc=1, device_id=inst_peer(d), device_id_type=pl.DeviceIdType.MESH)
    for db, ds in others:
        pl.semaphore_signal(barrier, inc=1, device_id=ring_peer(db, ds), device_id_type=pl.DeviceIdType.MESH)
    pl.semaphore_wait(barrier, n - 1 + len(others))

    def remote(src, dst, send, recv, peer):
        return pltpu.make_async_remote_copy(src_ref=src, dst_ref=dst, send_sem=send, recv_sem=recv,
                                            device_id=peer, device_id_type=pl.DeviceIdType.MESH)

    def last_copy(d):
        return remote(last_ref, lastg.at[n - d - 1], last_s.at[d - 1], last_r.at[n - d - 1], inst_peer(d))

    def src_copy(d):
        return remote(src_ref, srcg.at[n - d - 1], src_s.at[d - 1], src_r.at[n - d - 1], inst_peer(d))

    def u_copy(t, d):
        return remote(uown.at[t], ugot.at[t, n - d - 1], u_s.at[t, d - 1], u_r.at[t, n - d - 1], inst_peer(d))

    def u_wait(t, d):
        remote(uown.at[t], ugot.at[t, d - 1], u_s.at[t, n - d - 1], u_r.at[t, d - 1], inst_peer(d)).wait_recv()
        for q in range(entries // 2):
            pair = ugot[t, d - 1, q]
            uloc[d - 1, 2 * q] = pair[:, :bs]
            uloc[d - 1, 2 * q + 1] = pair[:, bs:]

    def face_copies(t, par):
        head, tail = psi.at[par, 0, pl.ds(0, 2)], psi.at[par, 0, pl.ds(nb - 2, 2)]
        plan = ((tail, 1, 0), (head, nblk - 1, 0), (tail, 0, 1), (head, 0, nspan - 1))
        return [remote(part_, faces.at[t, k], face_s.at[t, k], face_r.at[t, k], ring_peer(db, ds))
                for k, (part_, db, ds) in enumerate(plan)]

    for d in range(1, n):
        last_copy(d).start()
    for d in range(1, n):
        src_copy(d).start()

    acc[entries] = jnp.zeros_like(acc[entries])

    def relayout(ref, d):
        def body(q, carry):
            pair = ref[:, pl.ds(pl.multiple_of(q * 2 * bs, 128), 2 * bs)]
            srcb[d, 2 * q] = pair[:, :bs]
            srcb[d, 2 * q + 1] = pair[:, bs:]
            return carry
        lax.fori_loop(0, nb // 2, body, 0)

    relayout(src_ref, 0)

    def own_copy(b, carry):
        psi[0, 0, b] = srcb[0, b]
        return carry
    lax.fori_loop(0, nb, own_copy, 0)

    rate = freq[0]

    def weight(di, dj):
        k = lax.rem(me + dj, n) - lax.rem(me + di, n)
        return rate * wt[k + n - 1]

    def products(t, par):
        sends = face_copies(t, par)
        for copy in sends:
            copy.start()
        for e in range(ni):
            x = psi[par, 0, icols[0, e]]
            prod = jnp.dot(x, jin[e], preferred_element_type=F32)
            acc[e] = prod + acc[prev[e]]
        for k, copy in enumerate(sends):
            copy.wait()
            floc[2 * k] = faces[t, k, 0]
            floc[2 * k + 1] = faces[t, k, 1]
        for e in range(nf):
            c = fcols[0, e]
            c = jnp.where(c < 4, fmap[jnp.minimum(c, 3)], c)
            beyond = ((c >= 4) & (c < 6) & (span == 0)) | ((c >= 6) & (span == nspan - 1))
            keep = jnp.where(beyond, 0.0, 1.0)
            x = floc[c]
            prod = jnp.dot(x, jout[e], preferred_element_type=F32) * keep
            acc[ni + e] = prod + acc[prev[ni + e]]

    def send_u(t):
        for q in range(entries // 2):
            uown[t, q] = jnp.concatenate([acc[2 * q], acc[2 * q + 1]], axis=1).astype(BF16)
        for d in range(1, n):
            u_copy(t, d).start()

    def block(t, par, b, first, final):
        nxt = 1 - par
        if first:
            now = [srcb[d, b].astype(F32) for d in range(1, n)]
        else:
            old = [psi[nxt, d, b].astype(F32) for d in range(n)]
            now = []
            for d in range(1, n):
                at = lasts[d - 1, 0, b]
                got = uloc[d - 1, jnp.minimum(at, entries - 1)].astype(F32)
                val = srcb[d, b].astype(F32) - jnp.where(at < entries, got, 0.0)
                for j in range(n):
                    if j != d:
                        val = val - weight(d, j) * old[j]
                val = val.astype(BF16)
                if not final:
                    psi[par, d, b] = val
                now.append(val.astype(F32))
        if first:
            for d in range(1, n):
                psi[par, d, b] = srcb[d, b]
        val = srcb[0, b].astype(F32) - acc[own_last(b)]
        spec = weight(0, 1) * now[0]
        for d in range(2, n):
            spec = spec + weight(0, d) * now[d - 1]
        val = (val - spec).astype(BF16)
        psi[nxt, 0, b] = val
        return val

    def own_last(b):
        return lasts[n - 1, 0, b]

    def update(t, par, first=False, final=False):
        def body(q, carry):
            lo = block(t, par, 2 * q, first, final)
            hi = block(t, par, 2 * q + 1, first, final)
            if final:
                out_ref[:, pl.ds(pl.multiple_of(q * 2 * bs, 128), 2 * bs)] = jnp.concatenate([lo, hi], axis=1)
                res = []
                for m in range(nblk):
                    tot = carry[m]
                    tot = tot + lo.astype(F32) * wm_ref[2 * q, m:m + 1, :]
                    tot = tot + hi.astype(F32) * wm_ref[2 * q + 1, m:m + 1, :]
                    res.append(tot)
                return tuple(res)
            return carry
        init = tuple(jnp.zeros((src_ref.shape[0], bs), F32) for _ in range(nblk)) if final else 0
        return lax.fori_loop(0, nb // 2, body, init)

    products(0, 0)
    send_u(0)
    for d in range(1, n):
        last_copy(d).wait()
        src_copy(d).wait()
    local = [pltpu.make_async_copy(last_ref, lasts.at[n - 1], loc_sem.at[n - 1])]
    local += [pltpu.make_async_copy(lastg.at[d - 1], lasts.at[d - 1], loc_sem.at[d - 1]) for d in range(1, n)]
    for copy in local:
        copy.start()
    for copy in local:
        copy.wait()
    for d in range(1, n):
        relayout(srcg.at[d - 1], d)
    update(0, 0, first=True)

    def sweep(t, carry):
        par = lax.rem(t, 2)
        products(t, par)
        send_u(t)
        for d in range(1, n):
            u_wait(t - 1, d)
        update(t, par)
        return carry

    lax.fori_loop(1, ITERS - 1, sweep, 0)
    t_end = ITERS - 1
    products(t_end, t_end % 2)
    for d in range(1, n):
        u_wait(t_end - 1, d)
    totals = update(t_end, t_end % 2, final=True)

    for m in range(nblk):
        part[m] = jnp.broadcast_to(jnp.sum(totals[m], axis=1, keepdims=True), part.shape[1:])

    def slot(db, ds):
        return db * nspan + ds - 1

    copies = []
    for db, ds in others:
        mine = slot(db, ds)
        theirs = slot((nblk - db) % nblk, (nspan - ds) % nspan)
        copies.append(remote(part.at[lax.rem(blk + db, nblk)], partg.at[theirs], mod_s.at[mine], mod_r.at[theirs],
                             ring_peer(db, ds)))
    for copy in copies:
        copy.start()
    for copy in copies:
        copy.wait_send()
    total = part[blk]
    for k in range(len(others)):
        copies[k].wait_recv()
    for k in range(len(others)):
        total = total + partg[k]
    mod_ref[...] = total

    def drain(t, carry):
        for d in range(1, n):
            u_copy(t, d).wait_send()
        return carry
    lax.fori_loop(0, ITERS - 1, drain, 0)


def modal_weights(surf_mode, surf_row, surf_node, mode_shape, columns, bs):
    nblk = lax.axis_size("blk")
    lanes = 128
    shapes = lax.all_gather(mode_shape[0], "blk", axis=0, tiled=False)
    nodes = shapes.shape[1]
    e_node, e_row, e_mode = surf_node[0], surf_row[0], surf_mode[:, 0]
    hi = (e_node[:, None] // lanes == jnp.arange(nodes // lanes)[None]).astype(F32)
    lo = (e_node[:, None] % lanes == jnp.arange(lanes)[None]).astype(F32)
    hit = (e_mode[:, None] == jnp.arange(nblk)[None]).astype(F32)
    rows = jnp.einsum("eh,mhl->eml", hi, shapes.reshape(nblk, -1, lanes), precision=lax.Precision.HIGHEST)
    val = jnp.sum(rows * lo[:, None, :], axis=2) * hit
    blocks = (e_row[:, None] // bs == jnp.arange(columns // bs)[None]).astype(F32)
    lane = (e_row[:, None] % bs == jnp.arange(bs)[None]).astype(F32)
    left = (blocks[:, :, None] * jnp.pad(val, ((0, 0), (0, 8 - nblk)))[:, None, :]).reshape(e_row.shape[0], -1)
    return jnp.dot(left.T, lane, precision=lax.Precision.HIGHEST).reshape(columns // bs, 8, bs)


def on_device(source, jac_interior, interior_rows, interior_cols, jac_face, face_rows, face_cols, face_map,
              frequency, surf_mode, surf_row, surf_node, mode_shape):
    r, columns = source.shape[1:]
    ni, bs = jac_interior.shape[1:3]
    nf = jac_face.shape[1]
    nb = columns // bs
    entries = ni + nf
    n, nblk, nspan = lax.axis_size("inst"), lax.axis_size("blk"), lax.axis_size("span")
    ks = np.arange(-(n - 1), n)
    wt = np.array([0.0 if k == 0 else 0.5 * (-1.0) ** int(k) / math.sin(math.pi * k / n) for k in ks], np.float32)
    rows = jnp.concatenate([interior_rows[0], face_rows[0]])
    order = jnp.arange(entries)
    same = (rows[:, None] == rows[None, :]) & (order[None, :] < order[:, None])
    prev = jnp.max(jnp.where(same, order[None, :], -1), axis=1)
    prev = jnp.where(prev < 0, entries, prev).astype(jnp.int32)
    named = rows[None, :] == jnp.arange(128)[:, None]
    last = jnp.max(jnp.where(named, order[None, :], -1), axis=1)
    last = jnp.where(last < 0, entries, last).astype(jnp.int32)
    last = jnp.broadcast_to(last[None], (8, 128))
    wm = modal_weights(surf_mode, surf_row, surf_node, mode_shape, columns, bs)
    vmem = pl.BlockSpec(memory_space=pltpu.VMEM)
    smem = pl.BlockSpec(memory_space=pltpu.SMEM)
    dma = pltpu.SemaphoreType.DMA
    peers = nblk * nspan - 1
    adj, mod = pl.pallas_call(
        functools.partial(sweep_kernel, (n, nblk, nspan, ni, nf, nb, bs)),
        out_shape=(jax.ShapeDtypeStruct((r, columns), BF16), jax.ShapeDtypeStruct((r, 128), F32)),
        in_specs=[vmem, vmem, vmem, smem, smem, smem, smem, smem, smem, vmem, vmem],
        out_specs=(vmem, vmem),
        scratch_shapes=[
            pltpu.VMEM((n - 1, r, columns), BF16),
            pltpu.VMEM((n, nb, r, bs), BF16),
            pltpu.VMEM((2, n, nb, r, bs), BF16),
            pltpu.VMEM((entries + 1, r, bs), F32),
            pltpu.VMEM((ITERS - 1, entries // 2, r, 2 * bs), BF16),
            pltpu.VMEM((ITERS - 1, n - 1, entries // 2, r, 2 * bs), BF16),
            pltpu.VMEM((ITERS, 4, 2, r, bs), BF16),
            pltpu.VMEM((n - 1, 8, 128), jnp.int32),
            pltpu.SMEM((n, 8, 128), jnp.int32),
            pltpu.VMEM((nblk, r, 128), F32),
            pltpu.VMEM((peers, r, 128), F32),
            pltpu.VMEM((nf, r, bs), BF16),
            pltpu.VMEM((n - 1, entries, r, bs), BF16),
            dma((n - 1,)), dma((n - 1,)), dma((n - 1,)), dma((n - 1,)), dma((n,)),
            dma((ITERS, 4)), dma((ITERS, 4)),
            dma((ITERS - 1, n - 1)), dma((ITERS - 1, n - 1)),
            dma((peers,)), dma((peers,)),
        ],
        compiler_params=pltpu.CompilerParams(
            collective_id=0, has_side_effects=True, vmem_limit_bytes=58 * 2**20),
        name="sweeps",
    )(source[0], jac_interior[0], jac_face[0], interior_cols, face_cols, face_map, prev, frequency,
      jnp.asarray(wt), last, wm)
    return adj[None], mod[:, 0][None, None]


def solution(mesh):
    dev = ("blk", "span", "inst")
    return jax.shard_map(
        on_device,
        mesh=mesh,
        in_specs=(
            P("inst", None, ("blk", "span")),
            P(dev, None, None, None),
            P(dev, None),
            P(dev, None),
            P(dev, None, None, None),
            P(dev, None),
            P(dev, None),
            P(),
            P(),
            P(dev, None),
            P(dev, None),
            P(dev, None),
            P("blk", None),
        ),
        out_specs=(P("inst", None, ("blk", "span")), P("inst", "blk", None)),
        check_vma=False,
    )
```

```python
import functools
import math

import jax
import jax.numpy as jnp
import numpy as np
from jax import lax
from jax.experimental import pallas as pl
from jax.experimental.pallas import tpu as pltpu
from jax.sharding import PartitionSpec as P

ITERS = 6
F32 = jnp.float32
BF16 = jnp.bfloat16


def sweep_kernel(dims, src_ref, jin, jout, icols, fcols, fmap, prev, freq, wt, last_ref, wm_ref,
                 out_ref, mod_ref,
                 srcg, srcb, psi, acc, uown, ugot, faces, lastg, lasts, part, partg,
                 floc, uloc, src_s, src_r, last_s, last_r, loc_sem, face_s, face_r, uo_s, u_s, u_r, mod_s, mod_r):
    n, nblk, nspan, ni, nf, nb, bs = dims
    blk, span, me = lax.axis_index("blk"), lax.axis_index("span"), lax.axis_index("inst")
    entries = ni + nf

    def inst_peer(d):
        return {"inst": lax.rem(me + d, n)}

    def ring_peer(db, ds):
        return {"blk": lax.rem(blk + db, nblk), "span": lax.rem(span + ds, nspan)}

    others = [(db, ds) for db in range(nblk) for ds in range(nspan) if db or ds]
    barrier = pltpu.get_barrier_semaphore()
    for d in range(1, n):
        pl.semaphore_signal(barrier, inc=1, device_id=inst_peer(d), device_id_type=pl.DeviceIdType.MESH)
    for db, ds in others:
        pl.semaphore_signal(barrier, inc=1, device_id=ring_peer(db, ds), device_id_type=pl.DeviceIdType.MESH)
    pl.semaphore_wait(barrier, n - 1 + len(others))

    def remote(src, dst, send, recv, peer):
        return pltpu.make_async_remote_copy(src_ref=src, dst_ref=dst, send_sem=send, recv_sem=recv,
                                            device_id=peer, device_id_type=pl.DeviceIdType.MESH)

    def last_copy(d):
        return remote(last_ref, lastg.at[n - d - 1], last_s.at[d - 1], last_r.at[n - d - 1], inst_peer(d))

    def src_copy(d):
        return remote(src_ref, srcg.at[n - d - 1], src_s.at[d - 1], src_r.at[n - d - 1], inst_peer(d))

    def u_own(t, right):
        return remote(uown.at[t], ugot.at[t, n - 2 if right else 0], uo_s.at[t, int(right)],
                      u_r.at[t, n - 2 if right else 0], inst_peer(1 if right else n - 1))

    def u_on(t, d, right):
        to = max(d - 2, 0) if right else min(d, n - 2)
        return remote(ugot.at[t, d - 1], ugot.at[t, to], u_s.at[t, d - 1], u_r.at[t, to],
                      inst_peer(1 if right else n - 1))

    def u_here(t, d):
        return remote(uown.at[t], ugot.at[t, d - 1], u_s.at[t, d - 1], u_r.at[t, d - 1], inst_peer(1))

    def u_relay(t, o):
        @pl.when(me >= o)
        def _():
            u_here(t, n - o).wait_recv()
        if o < n - 1:
            @pl.when((me >= o) & (me < n - 1))
            def _():
                u_on(t, n - o, True).start()

        @pl.when(me + o <= n - 1)
        def _():
            u_here(t, o).wait_recv()
        if o < n - 1:
            @pl.when((me + o <= n - 1) & (me > 0))
            def _():
                u_on(t, o, False).start()

    def u_sent(t):
        @pl.when(me < n - 1)
        def _():
            u_own(t, True).wait_send()

        @pl.when(me > 0)
        def _():
            u_own(t, False).wait_send()
        for o in range(1, n - 1):
            @pl.when((me >= o) & (me < n - 1))
            def _(o=o):
                u_on(t, n - o, True).wait_send()

            @pl.when((me + o <= n - 1) & (me > 0))
            def _(o=o):
                u_on(t, o, False).wait_send()

    def u_unpack(t):
        for d in range(1, n):
            for q in range(entries // 2):
                pair = ugot[t, d - 1, q]
                uloc[d - 1, 2 * q] = pair[:, :bs]
                uloc[d - 1, 2 * q + 1] = pair[:, bs:]

    def face_copies(t, par):
        head, tail = psi.at[par, 0, pl.ds(0, 2)], psi.at[par, 0, pl.ds(nb - 2, 2)]
        plan = ((tail, 1, 0), (head, nblk - 1, 0), (tail, 0, 1), (head, 0, nspan - 1))
        return [remote(part_, faces.at[t, k], face_s.at[t, k], face_r.at[t, k], ring_peer(db, ds))
                for k, (part_, db, ds) in enumerate(plan)]

    for d in range(1, n):
        last_copy(d).start()
    for d in range(1, n):
        src_copy(d).start()

    acc[entries] = jnp.zeros_like(acc[entries])

    def relayout(ref, d):
        def body(q, carry):
            pair = ref[:, pl.ds(pl.multiple_of(q * 2 * bs, 128), 2 * bs)]
            srcb[d, 2 * q] = pair[:, :bs]
            srcb[d, 2 * q + 1] = pair[:, bs:]
            return carry
        lax.fori_loop(0, nb // 2, body, 0)

    relayout(src_ref, 0)

    def own_copy(b, carry):
        psi[0, 0, b] = srcb[0, b]
        return carry
    lax.fori_loop(0, nb, own_copy, 0)

    rate = freq[0]

    def weight(di, dj):
        k = lax.rem(me + dj, n) - lax.rem(me + di, n)
        return rate * wt[k + n - 1]

    def products(t, par):
        sends = face_copies(t, par)
        for copy in sends:
            copy.start()
        for e in range(ni):
            x = psi[par, 0, icols[0, e]]
            prod = jnp.dot(x, jin[e], preferred_element_type=F32)
            acc[e] = prod + acc[prev[e]]
        for k, copy in enumerate(sends):
            copy.wait()
            floc[2 * k] = faces[t, k, 0]
            floc[2 * k + 1] = faces[t, k, 1]
        for e in range(nf):
            c = fcols[0, e]
            c = jnp.where(c < 4, fmap[jnp.minimum(c, 3)], c)
            beyond = ((c >= 4) & (c < 6) & (span == 0)) | ((c >= 6) & (span == nspan - 1))
            keep = jnp.where(beyond, 0.0, 1.0)
            x = floc[c]
            prod = jnp.dot(x, jout[e], preferred_element_type=F32) * keep
            acc[ni + e] = prod + acc[prev[ni + e]]

    def send_u(t):
        for q in range(entries // 2):
            uown[t, q] = jnp.concatenate([acc[2 * q], acc[2 * q + 1]], axis=1).astype(BF16)

        @pl.when(me < n - 1)
        def _():
            u_own(t, True).start()

        @pl.when(me > 0)
        def _():
            u_own(t, False).start()

    def block(t, par, b, first, final):
        nxt = 1 - par
        if first:
            now = [srcb[d, b].astype(F32) for d in range(1, n)]
        else:
            old = [psi[nxt, d, b].astype(F32) for d in range(n)]
            now = []
            for d in range(1, n):
                at = lasts[d - 1, 0, b]
                got = uloc[d - 1, jnp.minimum(at, entries - 1)].astype(F32)
                val = srcb[d, b].astype(F32) - jnp.where(at < entries, got, 0.0)
                for j in range(n):
                    if j != d:
                        val = val - weight(d, j) * old[j]
                val = val.astype(BF16)
                if not final:
                    psi[par, d, b] = val
                now.append(val.astype(F32))
        if first:
            for d in range(1, n):
                psi[par, d, b] = srcb[d, b]
        val = srcb[0, b].astype(F32) - acc[own_last(b)]
        spec = weight(0, 1) * now[0]
        for d in range(2, n):
            spec = spec + weight(0, d) * now[d - 1]
        val = (val - spec).astype(BF16)
        psi[nxt, 0, b] = val
        return val

    def own_last(b):
        return lasts[n - 1, 0, b]

    def update(t, par, first=False, final=False):
        def body(q, carry):
            lo = block(t, par, 2 * q, first, final)
            hi = block(t, par, 2 * q + 1, first, final)
            if final:
                out_ref[:, pl.ds(pl.multiple_of(q * 2 * bs, 128), 2 * bs)] = jnp.concatenate([lo, hi], axis=1)
                res = []
                for m in range(nblk):
                    tot = carry[m]
                    tot = tot + lo.astype(F32) * wm_ref[2 * q, m:m + 1, :]
                    tot = tot + hi.astype(F32) * wm_ref[2 * q + 1, m:m + 1, :]
                    res.append(tot)
                return tuple(res)
            return carry
        init = tuple(jnp.zeros((src_ref.shape[0], bs), F32) for _ in range(nblk)) if final else 0
        return lax.fori_loop(0, nb // 2, body, init)

    products(0, 0)
    send_u(0)
    for d in range(1, n):
        last_copy(d).wait()
        src_copy(d).wait()
    local = [pltpu.make_async_copy(last_ref, lasts.at[n - 1], loc_sem.at[n - 1])]
    local += [pltpu.make_async_copy(lastg.at[d - 1], lasts.at[d - 1], loc_sem.at[d - 1]) for d in range(1, n)]
    for copy in local:
        copy.start()
    for copy in local:
        copy.wait()
    for d in range(1, n):
        relayout(srcg.at[d - 1], d)
    update(0, 0, first=True)

    def sweep(t, carry):
        par = lax.rem(t, 2)
        u_relay(t - 1, 1)
        products(t, par)
        for o in range(2, n):
            u_relay(t - 1, o)
        send_u(t)
        u_unpack(t - 1)
        update(t, par)
        return carry

    lax.fori_loop(1, ITERS - 1, sweep, 0)
    t_end = ITERS - 1
    u_relay(t_end - 1, 1)
    products(t_end, t_end % 2)
    for o in range(2, n):
        u_relay(t_end - 1, o)
    u_unpack(t_end - 1)
    totals = update(t_end, t_end % 2, final=True)

    for m in range(nblk):
        part[m] = jnp.broadcast_to(jnp.sum(totals[m], axis=1, keepdims=True), part.shape[1:])

    def slot(db, ds):
        return db * nspan + ds - 1

    copies = []
    for db, ds in others:
        mine = slot(db, ds)
        theirs = slot((nblk - db) % nblk, (nspan - ds) % nspan)
        copies.append(remote(part.at[lax.rem(blk + db, nblk)], partg.at[theirs], mod_s.at[mine], mod_r.at[theirs],
                             ring_peer(db, ds)))
    for copy in copies:
        copy.start()
    for copy in copies:
        copy.wait_send()
    total = part[blk]
    for k in range(len(others)):
        copies[k].wait_recv()
    for k in range(len(others)):
        total = total + partg[k]
    mod_ref[...] = total

    def drain(t, carry):
        u_sent(t)
        return carry
    lax.fori_loop(0, ITERS - 1, drain, 0)


def modal_weights(surf_mode, surf_row, surf_node, mode_shape, columns, bs):
    nblk = lax.axis_size("blk")
    lanes = 128
    shapes = lax.all_gather(mode_shape[0], "blk", axis=0, tiled=False)
    nodes = shapes.shape[1]
    e_node, e_row, e_mode = surf_node[0], surf_row[0], surf_mode[:, 0]
    hi = (e_node[:, None] // lanes == jnp.arange(nodes // lanes)[None]).astype(F32)
    lo = (e_node[:, None] % lanes == jnp.arange(lanes)[None]).astype(F32)
    hit = (e_mode[:, None] == jnp.arange(nblk)[None]).astype(F32)
    rows = jnp.einsum("eh,mhl->eml", hi, shapes.reshape(nblk, -1, lanes), precision=lax.Precision.HIGHEST)
    val = jnp.sum(rows * lo[:, None, :], axis=2) * hit
    blocks = (e_row[:, None] // bs == jnp.arange(columns // bs)[None]).astype(F32)
    lane = (e_row[:, None] % bs == jnp.arange(bs)[None]).astype(F32)
    left = (blocks[:, :, None] * jnp.pad(val, ((0, 0), (0, 8 - nblk)))[:, None, :]).reshape(e_row.shape[0], -1)
    return jnp.dot(left.T, lane, precision=lax.Precision.HIGHEST).reshape(columns // bs, 8, bs)


def on_device(source, jac_interior, interior_rows, interior_cols, jac_face, face_rows, face_cols, face_map,
              frequency, surf_mode, surf_row, surf_node, mode_shape):
    r, columns = source.shape[1:]
    ni, bs = jac_interior.shape[1:3]
    nf = jac_face.shape[1]
    nb = columns // bs
    entries = ni + nf
    n, nblk, nspan = lax.axis_size("inst"), lax.axis_size("blk"), lax.axis_size("span")
    ks = np.arange(-(n - 1), n)
    wt = np.array([0.0 if k == 0 else 0.5 * (-1.0) ** int(k) / math.sin(math.pi * k / n) for k in ks], np.float32)
    rows = jnp.concatenate([interior_rows[0], face_rows[0]])
    order = jnp.arange(entries)
    same = (rows[:, None] == rows[None, :]) & (order[None, :] < order[:, None])
    prev = jnp.max(jnp.where(same, order[None, :], -1), axis=1)
    prev = jnp.where(prev < 0, entries, prev).astype(jnp.int32)
    named = rows[None, :] == jnp.arange(128)[:, None]
    last = jnp.max(jnp.where(named, order[None, :], -1), axis=1)
    last = jnp.where(last < 0, entries, last).astype(jnp.int32)
    last = jnp.broadcast_to(last[None], (8, 128))
    wm = modal_weights(surf_mode, surf_row, surf_node, mode_shape, columns, bs)
    vmem = pl.BlockSpec(memory_space=pltpu.VMEM)
    smem = pl.BlockSpec(memory_space=pltpu.SMEM)
    dma = pltpu.SemaphoreType.DMA
    peers = nblk * nspan - 1
    adj, mod = pl.pallas_call(
        functools.partial(sweep_kernel, (n, nblk, nspan, ni, nf, nb, bs)),
        out_shape=(jax.ShapeDtypeStruct((r, columns), BF16), jax.ShapeDtypeStruct((r, 128), F32)),
        in_specs=[vmem, vmem, vmem, smem, smem, smem, smem, smem, smem, vmem, vmem],
        out_specs=(vmem, vmem),
        scratch_shapes=[
            pltpu.VMEM((n - 1, r, columns), BF16),
            pltpu.VMEM((n, nb, r, bs), BF16),
            pltpu.VMEM((2, n, nb, r, bs), BF16),
            pltpu.VMEM((entries + 1, r, bs), F32),
            pltpu.VMEM((ITERS - 1, entries // 2, r, 2 * bs), BF16),
            pltpu.VMEM((ITERS - 1, n - 1, entries // 2, r, 2 * bs), BF16),
            pltpu.VMEM((ITERS, 4, 2, r, bs), BF16),
            pltpu.VMEM((n - 1, 8, 128), jnp.int32),
            pltpu.SMEM((n, 8, 128), jnp.int32),
            pltpu.VMEM((nblk, r, 128), F32),
            pltpu.VMEM((peers, r, 128), F32),
            pltpu.VMEM((nf, r, bs), BF16),
            pltpu.VMEM((n - 1, entries, r, bs), BF16),
            dma((n - 1,)), dma((n - 1,)), dma((n - 1,)), dma((n - 1,)), dma((n,)),
            dma((ITERS, 4)), dma((ITERS, 4)),
            dma((ITERS - 1, 2)), dma((ITERS - 1, n - 1)), dma((ITERS - 1, n - 1)),
            dma((peers,)), dma((peers,)),
        ],
        compiler_params=pltpu.CompilerParams(
            collective_id=0, has_side_effects=True, vmem_limit_bytes=58 * 2**20),
        name="sweeps",
    )(source[0], jac_interior[0], jac_face[0], interior_cols, face_cols, face_map, prev, frequency,
      jnp.asarray(wt), last, wm)
    return adj[None], mod[:, 0][None, None]


def solution(mesh):
    dev = ("blk", "span", "inst")
    return jax.shard_map(
        on_device,
        mesh=mesh,
        in_specs=(
            P("inst", None, ("blk", "span")),
            P(dev, None, None, None),
            P(dev, None),
            P(dev, None),
            P(dev, None, None, None),
            P(dev, None),
            P(dev, None),
            P(),
            P(),
            P(dev, None),
            P(dev, None),
            P(dev, None),
            P("blk", None),
        ),
        out_specs=(P("inst", None, ("blk", "span")), P("inst", "blk", None)),
        check_vma=False,
    )
```
